32 devices in a mesh: lon: 8 (over y, x, core), head: 4 (over z).
Axes of the slice: x: 2, y: 2, z: 4, core: 2. Of those that a mesh axis runs over, the one named last changes fastest.
Arguments:
- latents: bfloat16 [3, 12, 64, 1024], P(None, 'head', 'lon'), may hold values from -16 to 16
- out_grad: bfloat16 [3, 12, 64, 1024], P(None, 'head', 'lon'), may hold values from -6 to 6
- qkv_weight: bfloat16 [16, 1024, 192], P('head'), as said below
- out_weight: bfloat16 [16, 64, 1024], replicated, may hold values from -0.1875 to 0.1875
Outputs:
- mixed: bfloat16 [3, 12, 64, 1024], P(None, 'head', 'lon')
- latent_grad: bfloat16 [3, 12, 64, 1024], P(None, 'head', 'lon')
- qkv_grad: float32 [16, 1024, 192], P('head')
The draws below stay inside these ranges and needn't reach their ends.
Inputs may be any that keep to these rules, and one draw needn't show every extreme that they name: `qkv_weight`: entries lie within -14 / sqrt(1024) and 14 / sqrt(1024).
All inputs are finite; a program needn't handle non-finite values.
Results may differ from the reference program's by a relative error of at most 0.024.
The reference program's roundings to bfloat16 on the way count: a program that leaves them out, or rounds other values in their place, can miss the bound.
Values may be sent and summed in bfloat16 or wider, within the bound.
A program may use at most 64 MiB of HBM per device.

```python
import jax
import jax.numpy as jnp
from jax import lax

D = 1024
HEADS = 16
HD = 64
LEV = 3
WIN_LAT = 6
WIN_LON = 8
LAT = 12
LON = 64


def draw_latents(key, part):
    key_base = jax.random.fold_in(key, 0)
    full_shape = (LEV, LAT, LON, D)
    normal_draw = jnp.clip(jax.random.normal(key_base, full_shape, jnp.float32), -5.0, 5.0)
    drawn = normal_draw
    return drawn.astype(jnp.bfloat16)


def draw_qkv_weight(key, part):
    key_query, key_keys, key_value = jax.random.split(key, 3)
    factor = D ** (-0.5)
    block_shape = (HEADS, D, HD)
    query_part = jnp.clip(jax.random.normal(key_query, block_shape, jnp.float32), -4.0, 4.0) * factor
    fresh_part = jnp.clip(jax.random.normal(key_keys, block_shape, jnp.float32), -4.0, 4.0) * factor
    value_portion = jnp.clip(jax.random.normal(key_value, block_shape, jnp.float32), -4.0, 4.0) * factor
    key_portion = fresh_part
    return jnp.concatenate([query_part, key_portion, value_portion], axis=-1).astype(jnp.bfloat16)


def block_levels(rng, shape, cuts, least, top_value):
    def one(axis_at, parts):
        draws = jax.random.uniform(jax.random.fold_in(jax.random.fold_in(rng, 6), axis_at), (parts,), jnp.float32, least / len(cuts), top_value / len(cuts))
        return jnp.repeat(jnp.exp(draws), shape[axis_at] // parts).reshape((-1,) + (1,) * (len(shape) - axis_at - 1))

    gain = one(*cuts[0])
    for cut in cuts[1:]:
        gain = gain * one(*cut)
    return gain


def normal_values(stream_key, dims, scale, bound, pieces=(), dtype=jnp.bfloat16):
    level = block_levels(stream_key, dims, pieces, -0.22, 0.18) if pieces else 1.0
    result = jax.random.normal(stream_key, dims, jnp.float32) * scale * level
    return jnp.minimum(jnp.maximum(result, -bound), bound).astype(dtype)


def setup_inputs(seed: int = 0) -> dict:
    seeds = jax.random.split(jax.random.key(seed), 5)
    latents = draw_latents(jax.random.fold_in(seeds[4], 71), 0)
    out_grad = normal_values(seeds[1], (LEV, LAT, LON, D), 1.0, 6.0, ((1, 4), (2, 8)))
    qkv_weight = draw_qkv_weight(jax.random.fold_in(seeds[4], 71), 0)
    out_weight = normal_values(seeds[3], (HEADS, HD, D), (HEADS * HD) ** -0.5, 0.1875)
    return {"latents": latents, "out_grad": out_grad, "qkv_weight": qkv_weight, "out_weight": out_weight}


MASKED = -1e30


def softmax_rows(query_rows, key_rows, valid, score_scale_factor):
    score_matrix = jnp.einsum("fud,fwd->fuw", query_rows.astype(jnp.float32), key_rows.astype(jnp.float32)) * score_scale_factor
    score_matrix = jnp.where(valid[:, None, :], score_matrix, MASKED)
    row_max = jnp.max(score_matrix, axis=-1, keepdims=True)
    powers = jnp.exp(score_matrix - row_max)
    return powers / jnp.sum(powers, axis=-1, keepdims=True)


def head_pass(latents, weight, outer_gradient):
    score_scale_factor = HD ** -0.5
    windows = LAT // WIN_LAT
    blocks = LON // WIN_LON
    key_cols = 2 * WIN_LON
    half_lat = WIN_LAT // 2
    half_lon = WIN_LON // 2
    flat = latents.reshape(-1, D)
    projected = jnp.dot(flat, weight, preferred_element_type=jnp.float32).astype(jnp.bfloat16)
    projected = projected.reshape(LEV, LAT, LON, 3 * HD)
    query_rows = projected[..., :HD].reshape(LEV, windows, WIN_LAT, blocks, WIN_LON, HD)
    query_rows = query_rows.transpose(1, 3, 0, 2, 4, 5).reshape(windows * blocks, LEV * WIN_LAT * WIN_LON, HD)
    col_index = ((WIN_LON * jnp.arange(blocks)[:, None] - WIN_LON // 2 + jnp.arange(key_cols)[None, :]) % LON).astype(jnp.int32)
    kv_cols = projected[..., HD:][:, :, col_index]
    padded = jnp.pad(kv_cols, ((0, 0), (half_lat, half_lat), (0, 0), (0, 0), (0, 0)))
    lower = padded[:, :LAT].reshape(LEV, windows, WIN_LAT, blocks, key_cols, 2 * HD)
    upper = padded[:, WIN_LAT:LAT + WIN_LAT].reshape(LEV, windows, WIN_LAT, blocks, key_cols, 2 * HD)
    joined = jnp.concatenate([lower, upper], axis=2)
    key_value_pairs = joined.transpose(1, 3, 0, 2, 4, 5).reshape(windows * blocks, LEV * 2 * WIN_LAT * key_cols, 2 * HD)
    lat_index = WIN_LAT * jnp.arange(windows)[:, None] - half_lat + jnp.arange(2 * WIN_LAT)[None, :]
    inside = (lat_index >= 0) & (lat_index < LAT)
    valid = jnp.broadcast_to(inside[:, None, None, :, None], (windows, blocks, LEV, 2 * WIN_LAT, key_cols))
    valid = valid.reshape(windows * blocks, -1)
    key_portion = key_value_pairs[..., :HD]
    value_portion = key_value_pairs[..., HD:]
    probs = softmax_rows(query_rows, key_portion, valid, score_scale_factor)
    probabilities_bfloat = probs.astype(jnp.bfloat16)
    attended_values = jnp.einsum("ucf,ufg->ucg", probabilities_bfloat.astype(jnp.float32), value_portion.astype(jnp.float32)).astype(jnp.bfloat16)
    attended_values = attended_values.reshape(windows, blocks, LEV, WIN_LAT, WIN_LON, HD).transpose(2, 0, 3, 1, 4, 5)
    attended_values = attended_values.reshape(LEV, LAT, LON, HD)
    window_gradient = outer_gradient.reshape(LEV, windows, WIN_LAT, blocks, WIN_LON, HD)
    window_gradient = window_gradient.transpose(1, 3, 0, 2, 4, 5).reshape(windows * blocks, LEV * WIN_LAT * WIN_LON, HD)
    probability_gradient = jnp.einsum("fud,fwd->fuw", window_gradient.astype(jnp.float32), value_portion.astype(jnp.float32))
    centre = jnp.sum(probs * probability_gradient, axis=-1, keepdims=True)
    score_gradient = (probs * (probability_gradient - centre)).astype(jnp.bfloat16)
    query_gradient = jnp.einsum("ucf,ufg->ucg", score_gradient.astype(jnp.float32), key_portion.astype(jnp.float32)) * score_scale_factor
    key_gradient = jnp.einsum("txd,txr->tdr", score_gradient.astype(jnp.float32), query_rows.astype(jnp.float32)) * score_scale_factor
    value_gradient = jnp.einsum("txd,txr->tdr", probabilities_bfloat.astype(jnp.float32), window_gradient.astype(jnp.float32))
    query_gradient = query_gradient.reshape(windows, blocks, LEV, WIN_LAT, WIN_LON, HD).transpose(2, 0, 3, 1, 4, 5)
    query_gradient = query_gradient.reshape(LEV, LAT, LON, HD)
    pair_grad = jnp.concatenate([key_gradient, value_gradient], axis=-1)
    pair_grad = pair_grad.reshape(windows, blocks, LEV, 2 * WIN_LAT, key_cols, 2 * HD).transpose(2, 0, 3, 1, 4, 5)
    lower_grad = pair_grad[:, :, :WIN_LAT].reshape(LEV, LAT, blocks, key_cols, 2 * HD)
    upper_grad = pair_grad[:, :, WIN_LAT:].reshape(LEV, LAT, blocks, key_cols, 2 * HD)
    summed = jnp.pad(lower_grad, ((0, 0), (0, WIN_LAT), (0, 0), (0, 0), (0, 0))) + jnp.pad(upper_grad, ((0, 0), (WIN_LAT, 0), (0, 0), (0, 0), (0, 0)))
    trimmed = summed[:, half_lat:half_lat + LAT]
    rounded = lax.optimization_barrier(trimmed.astype(jnp.bfloat16)).astype(jnp.float32)
    col_pos = jnp.arange(key_cols)
    inner = (col_pos >= half_lon) & (col_pos < half_lon + WIN_LON)
    trimmed = jnp.where(inner[None, None, None, :, None], trimmed, rounded)
    kv_grad = jnp.zeros((LEV, LAT, LON, 2 * HD), jnp.float32).at[:, :, col_index].add(trimmed)
    projected_grad = jnp.concatenate([query_gradient, kv_grad], axis=-1).astype(jnp.bfloat16)
    return attended_values, projected_grad


def reference(latents, out_grad, qkv_weight, out_weight):
    flat = latents.reshape(-1, D)
    grad_flat = out_grad.reshape(-1, D)
    out_flat = out_weight.reshape(HEADS * HD, D)
    attended_grad = jnp.dot(grad_flat, out_flat.T, preferred_element_type=jnp.float32).astype(jnp.bfloat16)
    attended_grad = attended_grad.reshape(LEV, LAT, LON, HEADS, HD).transpose(3, 0, 1, 2, 4)

    def per_head(carry, pack):
        mixed_sum, latent_sum = carry
        weight, out_rows, outer_gradient = pack
        attended_values, projected_grad = head_pass(latents, weight, outer_gradient)
        mixed_sum = mixed_sum + jnp.dot(attended_values.reshape(-1, HD), out_rows, preferred_element_type=jnp.float32)
        grad_rows = projected_grad.reshape(-1, 3 * HD)
        latent_sum = latent_sum + jnp.dot(grad_rows, weight.T, preferred_element_type=jnp.float32)
        head_grad = jnp.dot(flat.T, grad_rows, preferred_element_type=jnp.float32)
        return (mixed_sum, latent_sum), head_grad

    start = (jnp.zeros((flat.shape[0], D), jnp.float32), jnp.zeros((flat.shape[0], D), jnp.float32))
    (mixed_sum, latent_sum), qkv_grad = lax.scan(per_head, start, (qkv_weight, out_weight, attended_grad))
    mixed = mixed_sum.astype(jnp.bfloat16).reshape(LEV, LAT, LON, D)
    latent_grad = latent_sum.astype(jnp.bfloat16).reshape(LEV, LAT, LON, D)
    return mixed, latent_grad, qkv_grad
```

```python
import functools

import jax
import jax.numpy as jnp
import numpy as np
from jax import lax
from jax.experimental import pallas as pl
from jax.experimental.pallas import tpu as pltpu
from jax.sharding import PartitionSpec as P

WIN_LAT = 6
WIN_LON = 8
MASKED = -1e30
ROW_TILE = 16

F32 = jnp.float32
BF16 = jnp.bfloat16


def dot(a, b, dims=(1, 0)):
    return lax.dot_general(
        a, b, (((dims[0],), (dims[1],)), ((), ())), preferred_element_type=F32
    )


def remote(src, dst, sems, index, axis, device):
    send, recv = sems
    return pltpu.make_async_remote_copy(
        src_ref=src,
        dst_ref=dst,
        send_sem=send.at[index],
        recv_sem=recv.at[index],
        device_id={axis: device},
        device_id_type=pl.DeviceIdType.MESH,
    )


def kernel(
    dims,
    lat_ref,
    grad_ref,
    w_ref,
    out_w_ref,
    pick_ref,
    bias_ref,
    mixed_ref,
    latent_ref,
    qkv_ref,
    band,
    d_out,
    grad_send,
    query,
    keys,
    halo_send,
    acc,
    halo_grad_send,
    halo_grad,
    own_grad,
    attended,
    tokens,
    proj_grad,
    part,
    half_in,
    half_sum,
    chips_in,
    lat_send,
    lat_in,
    *sems,
):
    groups, count, heads, width, block, windows, edge = dims
    rows = groups * block
    win_rows = rows // windows
    scale = width ** (-0.5)
    gather_s, grad_s, att_s, lat_s, halo_s, hgrad_s, half_s, chip_s, all_s, pair_s = [
        (sems[2 * i], sems[2 * i + 1]) for i in range(10)
    ]
    me = lax.axis_index("lon")
    row = lax.axis_index("head")
    chips = count // 2
    core = lax.rem(me, 2)
    chip = lax.div(me, 2)
    pair = me + 1 - 2 * core
    east = lax.rem(me + 1, count)
    west = lax.rem(me + count - 1, count)
    pending = []

    def partner(d):
        return lax.rem(row + d, groups)

    def chip_at(d):
        return lax.rem(chip + d, chips)

    def block_of(g):
        return pl.ds(pl.multiple_of(g * block, ROW_TILE), block)

    offsets = sorted({1, count - 1} | set(range(2, count, 2)))
    barrier = pltpu.get_barrier_semaphore()
    for d in range(1, groups):
        pl.semaphore_signal(
            barrier, inc=1, device_id={"head": partner(d)}, device_id_type=pl.DeviceIdType.MESH
        )
    for d in offsets:
        pl.semaphore_signal(
            barrier,
            inc=1,
            device_id={"lon": lax.rem(me + d, count)},
            device_id_type=pl.DeviceIdType.MESH,
        )
    pl.semaphore_wait(barrier, groups - 1 + len(offsets))

    def launch(copy):
        copy.start()
        pending.append(copy)
        return copy

    mine = block_of(row)
    gathers = [
        launch(remote(lat_ref, band.at[mine], gather_s, d - 1, "head", partner(d)))
        for d in range(1, groups)
    ]
    band[mine, :] = lat_ref[...]

    cols = heads * width
    grads = []
    for d in range(1, groups + 1):
        g = partner(d)
        some = dot(
            grad_ref[...], out_w_ref[pl.ds(pl.multiple_of(g * cols, ROW_TILE), cols), :], (1, 1)
        ).astype(BF16)
        if d < groups:
            grad_send[d - 1] = some
            grads.append(
                launch(remote(grad_send.at[d - 1], d_out.at[mine], grad_s, d - 1, "head", g))
            )
        else:
            d_out[mine, :] = some
    for copy in gathers:
        copy.wait_recv()

    halos = []
    for h in range(heads):
        projected = dot(band[...], w_ref[h]).astype(BF16)
        query[h] = projected[:, :width]
        pairs = projected[:, width:]
        keys[h, 0:rows, :] = pairs
        copies = []
        for side, device in ((0, east), (1, west)):
            halo_send[side, h] = dot(pick_ref[side], pairs).astype(BF16)
            copies.append(
                launch(
                    remote(
                        halo_send.at[side, h],
                        keys.at[h, pl.ds(rows + side * edge, edge)],
                        halo_s,
                        (side, h),
                        "lon",
                        device,
                    )
                )
            )
        halos.append(copies)
    for copy in grads:
        copy.wait_recv()

    returns = []
    for h in range(heads):
        for copy in halos[h]:
            copy.wait_recv()
        acc[...] = jnp.zeros_like(acc)

        def window(w, carry):
            here = pl.ds(pl.multiple_of(w * win_rows, ROW_TILE), win_rows)
            q = query[h, here, :]
            k = keys[h, :, 0:width]
            v = keys[h, :, width : 2 * width]
            scores = dot(q, k, (1, 1)) * scale + bias_ref[w]
            powers = jnp.exp(scores - jnp.max(scores, axis=-1, keepdims=True))
            probs = powers / jnp.sum(powers, axis=-1, keepdims=True)
            probs_b = probs.astype(BF16)
            attended[here, h * width : (h + 1) * width] = dot(probs_b, v).astype(BF16)
            outer = d_out[here, h * width : (h + 1) * width]
            prob_grad = dot(outer, v, (1, 1))
            centre = jnp.sum(probs * prob_grad, axis=-1, keepdims=True)
            score_grad = (probs * (prob_grad - centre)).astype(BF16)
            proj_grad[here, 3 * h * width : (3 * h + 1) * width] = (
                dot(score_grad, k) * scale
            ).astype(BF16)
            acc[:, 0:width] += dot(score_grad, q, (0, 0)) * scale
            acc[:, width : 2 * width] += dot(probs_b, outer, (0, 0))
            return carry

        lax.fori_loop(0, windows, window, 0)
        own_grad[h] = acc[0:rows, :]
        copies = []
        for side, device in ((0, west), (1, east)):
            halo_grad_send[side, h] = acc[
                rows + side * edge : rows + (side + 1) * edge, :
            ].astype(BF16)
            copies.append(
                launch(
                    remote(
                        halo_grad_send.at[side, h],
                        halo_grad.at[side, h],
                        hgrad_s,
                        (side, h),
                        "lon",
                        device,
                    )
                )
            )
        returns.append(copies)

    sent = []
    for d in range(1, groups):
        sent.append(
            launch(
                remote(
                    attended.at[block_of(partner(d))],
                    tokens.at[row],
                    att_s,
                    d - 1,
                    "head",
                    partner(d),
                )
            )
        )
    tokens[row] = attended[mine, :]

    for h in range(heads):
        for copy in returns[h]:
            copy.wait_recv()
        total = own_grad[h]
        for side in range(2):
            total += dot(pick_ref[side], halo_grad[side, h], (0, 0))
        proj_grad[:, (3 * h + 1) * width : 3 * (h + 1) * width] = total.astype(BF16)

    depth = band.shape[1]
    half = depth // 2
    step = min(half, 256)

    def qkv_half(which):
        def one(i, carry):
            at = pl.multiple_of(which * half + i * step, 128)
            part[pl.ds(at, step), :] = dot(
                band[:, pl.ds(at, step)], proj_grad[...], (0, 0)
            ).astype(BF16)
            return carry

        lax.fori_loop(0, half // step, one, 0)

    qkv_half(1 - core)
    theirs = pl.ds(pl.multiple_of((1 - core) * half, ROW_TILE), half)
    ours = pl.ds(pl.multiple_of(core * half, ROW_TILE), half)
    halves = launch(remote(part.at[theirs], half_in, half_s, 0, "lon", pair))
    qkv_half(core)

    wide = min(depth, 256)

    def latent(i, carry):
        at = pl.ds(pl.multiple_of(i * wide, 128), wide)
        total = jnp.zeros((rows, wide), F32)
        for h in range(heads):
            total += dot(
                proj_grad[:, 3 * h * width : 3 * (h + 1) * width], w_ref[h, at, :], (1, 1)
            )
        lat_send[:, at] = total.astype(BF16)
        return carry

    lax.fori_loop(0, depth // wide, latent, 0)
    lats = [
        launch(
            remote(
                lat_send.at[block_of(partner(d))], lat_in.at[d - 1], lat_s, d - 1, "head", partner(d)
            )
        )
        for d in range(1, groups)
    ]

    halves.wait_recv()
    piece = half // chips
    half_sum[...] = (part[ours, :].astype(F32) + half_in[...].astype(F32)).astype(BF16)

    def piece_of(t):
        return pl.ds(pl.multiple_of(t * piece, ROW_TILE), piece)

    exchanged = [
        launch(
            remote(
                half_sum.at[piece_of(chip_at(d))],
                chips_in.at[d - 1],
                chip_s,
                d - 1,
                "lon",
                2 * chip_at(d) + core,
            )
        )
        for d in range(1, chips)
    ]

    for copy in sent:
        copy.wait_recv()
    mixed = jnp.zeros((block, depth), F32)
    for g in range(groups):
        mixed += dot(tokens[g], out_w_ref[g * cols : (g + 1) * cols, :])
    mixed_ref[...] = mixed.astype(BF16)

    for copy in exchanged:
        copy.wait_recv()
    total = half_sum[piece_of(chip), :].astype(F32)
    for d in range(1, chips):
        total += chips_in[d - 1].astype(F32)

    def result_of(t):
        return pl.ds(pl.multiple_of(core * half + t * piece, ROW_TILE), piece)

    final = result_of(chip)
    qkv_ref[final, :] = total.astype(BF16)
    spread = [
        launch(
            remote(
                qkv_ref.at[final], qkv_ref.at[final], all_s, d - 1, "lon", 2 * chip_at(d) + core
            )
        )
        for d in range(1, chips)
    ]
    shared = [launch(remote(qkv_ref.at[final], qkv_ref.at[final], pair_s, 0, "lon", pair))]

    for copy in lats:
        copy.wait_recv()
    total = lat_send[mine, :].astype(F32)
    for d in range(1, groups):
        total += lat_in[d - 1].astype(F32)
    latent_ref[...] = total.astype(BF16)

    for d in range(1, chips):
        spread[d - 1].wait_recv()
        came = result_of(lax.rem(chip + chips - d, chips))
        shared.append(launch(remote(qkv_ref.at[came], qkv_ref.at[came], pair_s, d, "lon", pair)))
    for copy in shared:
        copy.wait_recv()
    for copy in pending:
        copy.wait_send()


def tables(levels, lat_dev, groups, columns, windows, block):
    half = columns // 2
    lat_rows = lat_dev * groups
    edge = lat_rows * levels * half
    pick = np.zeros((2, edge, groups * block), np.float32)
    key_lat = np.full((groups * block,), -(10**6))
    for g in range(groups):
        for r in range(lat_dev):
            for level in range(levels):
                base = g * block + (r * levels + level) * columns
                key_lat[base : base + columns] = g * lat_dev + r
                at = ((g * lat_dev + r) * levels + level) * half
                for c in range(half):
                    pick[0, at + c, base + columns - half + c] = 1
                    pick[1, at + c, base + c] = 1
    edge_lat = np.repeat(np.arange(lat_rows), levels * half)
    lat = np.concatenate([key_lat, edge_lat, edge_lat])
    low = WIN_LAT * np.arange(windows)[:, None] - WIN_LAT // 2
    inside = (lat[None] >= low) & (lat[None] < low + 2 * WIN_LAT)
    bias = np.where(inside & (lat[None] >= 0), 0.0, MASKED).astype(np.float32)
    return pick, bias[:, None, :], edge


def body(latents, out_grad, qkv_weight, out_weight):
    levels, lat_dev, columns, model_width = latents.shape
    groups = lax.axis_size("head")
    count = lax.axis_size("lon")
    heads = qkv_weight.shape[0]
    width = out_weight.shape[1]
    windows = lat_dev * groups // WIN_LAT
    valid = levels * lat_dev * columns
    block = -(-valid // ROW_TILE) * ROW_TILE
    rows = groups * block
    pick, bias, edge = tables(levels, lat_dev, groups, columns, windows, block)
    keys = rows + 2 * edge
    cols = heads * width
    chips = count // 2
    half = model_width // 2

    def packed(x):
        x = x.transpose(1, 0, 2, 3).reshape(valid, model_width)
        return jnp.pad(x, ((0, block - valid), (0, 0)))

    def unpacked(x):
        return x[:valid].reshape(lat_dev, levels, columns, model_width).transpose(1, 0, 2, 3)

    dma = pltpu.SemaphoreType.DMA
    shapes = [
        (groups - 1,),
        (groups - 1,),
        (groups - 1,),
        (groups - 1,),
        (2, heads),
        (2, heads),
        (1,),
        (chips - 1,),
        (chips - 1,),
        (chips,),
    ]
    vmem = pl.BlockSpec(memory_space=pltpu.VMEM)
    mixed, latent_grad, qkv = pl.pallas_call(
        functools.partial(kernel, (groups, count, heads, width, block, windows, edge)),
        out_shape=(
            jax.ShapeDtypeStruct((block, model_width), BF16),
            jax.ShapeDtypeStruct((block, model_width), BF16),
            jax.ShapeDtypeStruct((model_width, 3 * cols), BF16),
        ),
        in_specs=[vmem] * 6,
        out_specs=(vmem,) * 3,
        scratch_shapes=[
            pltpu.VMEM((rows, model_width), BF16),
            pltpu.VMEM((rows, cols), BF16),
            pltpu.VMEM((groups - 1, block, cols), BF16),
            pltpu.VMEM((heads, rows, width), BF16),
            pltpu.VMEM((heads, keys, 2 * width), BF16),
            pltpu.VMEM((2, heads, edge, 2 * width), BF16),
            pltpu.VMEM((keys, 2 * width), F32),
            pltpu.VMEM((2, heads, edge, 2 * width), BF16),
            pltpu.VMEM((2, heads, edge, 2 * width), BF16),
            pltpu.VMEM((heads, rows, 2 * width), F32),
            pltpu.VMEM((rows, cols), BF16),
            pltpu.VMEM((groups, block, cols), BF16),
            pltpu.VMEM((rows, 3 * cols), BF16),
            pltpu.VMEM((model_width, 3 * cols), BF16),
            pltpu.VMEM((half, 3 * cols), BF16),
            pltpu.VMEM((half, 3 * cols), BF16),
            pltpu.VMEM((chips - 1, half // chips, 3 * cols), BF16),
            pltpu.VMEM((rows, model_width), BF16),
            pltpu.VMEM((groups - 1, block, model_width), BF16),
        ]
        + [dma(s) for s in shapes for _ in range(2)],
        compiler_params=pltpu.CompilerParams(
            collective_id=0, has_side_effects=True, vmem_limit_bytes=56 * 1024 * 1024
        ),
    )(
        packed(latents),
        packed(out_grad),
        qkv_weight,
        out_weight.reshape(-1, model_width),
        jnp.asarray(pick, BF16),
        jnp.asarray(bias),
    )
    qkv_grad = qkv.reshape(model_width, heads, 3 * width).transpose(1, 0, 2).astype(F32)
    return unpacked(mixed), unpacked(latent_grad), qkv_grad


def solution(mesh):
    placed = (
        P(None, "head", "lon", None),
        P(None, "head", "lon", None),
        P("head", None, None),
        P(),
    )
    return jax.shard_map(
        body,
        mesh=mesh,
        in_specs=placed,
        out_specs=(
            P(None, "head", "lon", None),
            P(None, "head", "lon", None),
            P("head", None, None),
        ),
        check_vma=False,
    )
```

```python
import functools

import jax
import jax.numpy as jnp
import numpy as np
from jax import lax
from jax.experimental import pallas as pl
from jax.experimental.pallas import tpu as pltpu
from jax.sharding import PartitionSpec as P

WIN_LAT = 6
WIN_LON = 8
MASKED = -1e30
ROW_TILE = 16

F32 = jnp.float32
BF16 = jnp.bfloat16


def dot(a, b, dims=(1, 0)):
    return lax.dot_general(
        a, b, (((dims[0],), (dims[1],)), ((), ())), preferred_element_type=F32
    )


def remote(src, dst, sems, index, axis, device):
    send, recv = sems
    return pltpu.make_async_remote_copy(
        src_ref=src,
        dst_ref=dst,
        send_sem=send.at[index],
        recv_sem=recv.at[index],
        device_id={axis: device},
        device_id_type=pl.DeviceIdType.MESH,
    )


def kernel(
    dims,
    lat_ref,
    grad_ref,
    w_ref,
    out_w_ref,
    pick_ref,
    bias_ref,
    mixed_ref,
    latent_ref,
    qkv_ref,
    band,
    d_out,
    grad_send,
    query,
    keys,
    halo_send,
    soft,
    hard,
    halo_grad_send,
    halo_grad,
    own_grad,
    attended,
    tokens,
    proj_grad,
    part,
    half_in,
    half_sum,
    chips_in,
    lat_send,
    lat_in,
    *sems,
):
    groups, count, heads, width, block, windows, edge = dims
    levels, lat_dev, columns, depth = lat_ref.shape
    cols = heads * width
    rows = groups * block
    win_rows = rows // windows
    scale = width ** (-0.5)
    gather_s, grad_s, att_s, lat_s, halo_s, hgrad_s, half_s, chip_s, all_s, pair_s = [
        (sems[2 * i], sems[2 * i + 1]) for i in range(10)
    ]
    me = lax.axis_index("lon")
    row = lax.axis_index("head")
    chips = count // 2
    core = lax.rem(me, 2)
    chip = lax.div(me, 2)
    pair = me + 1 - 2 * core
    east = lax.rem(me + 1, count)
    west = lax.rem(me + count - 1, count)
    pending = []

    def partner(d):
        return lax.rem(row + d, groups)

    def chip_at(d):
        return lax.rem(chip + d, chips)

    def block_of(g):
        return pl.ds(pl.multiple_of(g * block, ROW_TILE), block)

    mine = block_of(row)
    def packed(ref):
        parts = [ref[level, r].astype(F32) for r in range(lat_dev) for level in range(levels)]
        if block > len(parts) * columns:
            parts.append(jnp.zeros((block - len(parts) * columns, depth), F32))
        return jnp.concatenate(parts, axis=0).astype(BF16)

    def unpacked(ref, value):
        for r in range(lat_dev):
            for level in range(levels):
                at = (r * levels + level) * columns
                ref[level, r] = value[at : at + columns].astype(BF16)

    offsets = sorted({1, count - 1} | set(range(2, count, 2)))
    barrier = pltpu.get_barrier_semaphore()
    for d in range(1, groups):
        pl.semaphore_signal(
            barrier, inc=1, device_id={"head": partner(d)}, device_id_type=pl.DeviceIdType.MESH
        )
    for d in offsets:
        pl.semaphore_signal(
            barrier,
            inc=1,
            device_id={"lon": lax.rem(me + d, count)},
            device_id_type=pl.DeviceIdType.MESH,
        )
    band[mine, :] = packed(lat_ref)
    pl.semaphore_wait(barrier, groups - 1 + len(offsets))

    def launch(copy):
        copy.start()
        pending.append(copy)
        return copy

    gathers = [
        launch(remote(band.at[mine], band.at[mine], gather_s, d - 1, "head", partner(d)))
        for d in range(1, groups)
    ]
    out_grad = packed(grad_ref)
    grads = []
    for d in range(1, groups + 1):
        g = partner(d)
        some = dot(
            out_grad, out_w_ref[pl.ds(pl.multiple_of(g * cols, ROW_TILE), cols), :], (1, 1)
        ).astype(BF16)
        if d < groups:
            grad_send[d - 1] = some
            grads.append(
                launch(remote(grad_send.at[d - 1], d_out.at[mine], grad_s, d - 1, "head", g))
            )
        else:
            d_out[mine, :] = some
    for copy in gathers:
        copy.wait_recv()

    halos = []
    projected = dot(band[...], w_ref[...], (1, 1)).astype(BF16)
    for h in range(heads):
        base = 3 * h * width
        query[h] = (projected[:, base : base + width].astype(F32) * scale).astype(BF16)
        pairs = projected[:, base + width : base + 3 * width]
        keys[h, 0:rows, :] = pairs
        copies = []
        for side, device in ((0, east), (1, west)):
            halo_send[side, h] = dot(pick_ref[side], pairs).astype(BF16)
            copies.append(
                launch(
                    remote(
                        halo_send.at[side, h],
                        keys.at[h, pl.ds(rows + side * edge, edge)],
                        halo_s,
                        (side, h),
                        "lon",
                        device,
                    )
                )
            )
        halos.append(copies)
    for copy in grads:
        copy.wait_recv()

    for copies in halos:
        for copy in copies:
            copy.wait_recv()

    def window(some, w):
        here = pl.ds(pl.multiple_of(w * win_rows, ROW_TILE), win_rows)
        for h in some:
            lanes = slice(h * width, (h + 1) * width)
            k = keys[h, :, 0:width]
            v = keys[h, :, width : 2 * width]
            scores = dot(query[h, here, :], k, (1, 1)) + bias_ref[w]
            prob_grad = dot(d_out[here, lanes], v, (1, 1))
            powers = jnp.exp(scores - jnp.max(scores, axis=-1, keepdims=True))
            probs = powers * (1.0 / jnp.sum(powers, axis=-1, keepdims=True))
            probs_b = probs.astype(BF16)
            hard[h, here, :] = probs_b
            centre = jnp.sum(probs * prob_grad, axis=-1, keepdims=True)
            score_grad = (probs * (prob_grad - centre)).astype(BF16)
            soft[h, here, :] = score_grad
            attended[here, lanes] = dot(probs_b, v).astype(BF16)
            proj_grad[here, 3 * h * width : (3 * h + 1) * width] = (
                dot(score_grad, k) * scale
            ).astype(BF16)

    returns = []
    for first in range(0, heads, 2):
        some = range(first, min(first + 2, heads))
        if windows <= 2:
            for w in range(windows):
                window(some, w)
        else:
            lax.fori_loop(0, windows, lambda w, c, some=some: (window(some, w), c)[1], 0)
        for h in some:
            whole = jnp.concatenate(
                [
                    dot(soft[h], query[h], (0, 0)),
                    dot(hard[h], d_out[:, h * width : (h + 1) * width], (0, 0)),
                ],
                axis=1,
            )
            own_grad[h] = whole[0:rows, :]
            for side in range(2):
                halo_grad_send[side, h] = whole[
                    rows + side * edge : rows + (side + 1) * edge, :
                ].astype(BF16)
        for h in some:
            copies = []
            for side, device in ((0, west), (1, east)):
                copies.append(
                    launch(
                        remote(
                            halo_grad_send.at[side, h],
                            halo_grad.at[side, h],
                            hgrad_s,
                            (side, h),
                            "lon",
                            device,
                        )
                    )
                )
            returns.append(copies)

    sent = []
    for d in range(1, groups):
        sent.append(
            launch(
                remote(
                    attended.at[block_of(partner(d))],
                    tokens.at[row],
                    att_s,
                    d - 1,
                    "head",
                    partner(d),
                )
            )
        )
    tokens[row] = attended[mine, :]

    for h in range(heads):
        for copy in returns[h]:
            copy.wait_recv()
        total = own_grad[h]
        for side in range(2):
            total += dot(pick_ref[side], halo_grad[side, h], (0, 0))
        proj_grad[:, (3 * h + 1) * width : 3 * (h + 1) * width] = total.astype(BF16)

    lanes = part.shape[2]
    lane_blocks = half_in.shape[0]
    wide = 2 * lanes

    def qkv_half(which):
        def one(i, carry):
            at = which * lane_blocks + 2 * i
            found = dot(
                proj_grad[...], band[:, pl.ds(pl.multiple_of(at * lanes, wide), wide)], (0, 0)
            ).astype(BF16)
            part[at] = found[:, :lanes]
            part[at + 1] = found[:, lanes:]
            return carry

        lax.fori_loop(0, lane_blocks // 2, one, 0)

    qkv_half(1 - core)
    halves = launch(
        remote(part.at[pl.ds((1 - core) * lane_blocks, lane_blocks)], half_in, half_s, 0, "lon", pair)
    )
    qkv_half(core)

    def latent(i, carry):
        at = pl.ds(pl.multiple_of(i * wide, wide), wide)
        lat_send[:, at] = dot(proj_grad[...], w_ref[:, at]).astype(BF16)
        return carry

    lax.fori_loop(0, depth // wide, latent, 0)
    lats = [
        launch(
            remote(
                lat_send.at[block_of(partner(d))], lat_in.at[d - 1], lat_s, d - 1, "head", partner(d)
            )
        )
        for d in range(1, groups)
    ]

    halves.wait_recv()
    ours = pl.ds(core * lane_blocks, lane_blocks)
    half_sum[...] = (part[ours].astype(F32) + half_in[...].astype(F32)).astype(BF16)
    piece = chips_in.shape[1]

    def piece_of(t):
        return lax.rem(t, lane_blocks), pl.ds(
            pl.multiple_of(lax.div(t, lane_blocks) * piece, ROW_TILE), piece
        )

    def result_of(t):
        lane, here = piece_of(t)
        at = (core * lane_blocks + lane) * lanes
        return here, pl.ds(pl.multiple_of(at, lanes), lanes)

    exchanged = [
        launch(
            remote(
                half_sum.at[piece_of(chip_at(d))],
                chips_in.at[d - 1],
                chip_s,
                d - 1,
                "lon",
                2 * chip_at(d) + core,
            )
        )
        for d in range(1, chips)
    ]

    for copy in sent:
        copy.wait_recv()
    mixed = jnp.zeros((block, depth), F32)
    for g in range(groups):
        mixed += dot(tokens[g], out_w_ref[g * cols : (g + 1) * cols, :])
    unpacked(mixed_ref, mixed)

    for copy in exchanged:
        copy.wait_recv()
    total = half_sum[piece_of(chip)].astype(F32)
    for d in range(1, chips):
        total += chips_in[d - 1].astype(F32)

    final = result_of(chip)
    qkv_ref[final] = total.astype(BF16)
    spread = [
        launch(
            remote(
                qkv_ref.at[final], qkv_ref.at[final], all_s, d - 1, "lon", 2 * chip_at(d) + core
            )
        )
        for d in range(1, chips)
    ]
    shared = [launch(remote(qkv_ref.at[final], qkv_ref.at[final], pair_s, 0, "lon", pair))]

    for copy in lats:
        copy.wait_recv()
    total = lat_send[mine, :].astype(F32)
    for d in range(1, groups):
        total += lat_in[d - 1].astype(F32)
    unpacked(latent_ref, total)

    for d in range(1, chips):
        spread[d - 1].wait_recv()
        came = result_of(lax.rem(chip + chips - d, chips))
        shared.append(launch(remote(qkv_ref.at[came], qkv_ref.at[came], pair_s, d, "lon", pair)))
    for copy in shared:
        copy.wait_recv()
    for copy in pending:
        copy.wait_send()


def tables(levels, lat_dev, groups, columns, windows, block):
    half = columns // 2
    lat_rows = lat_dev * groups
    edge = lat_rows * levels * half
    pick = np.zeros((2, edge, groups * block), np.float32)
    key_lat = np.full((groups * block,), -(10**6))
    for g in range(groups):
        for r in range(lat_dev):
            for level in range(levels):
                base = g * block + (r * levels + level) * columns
                key_lat[base : base + columns] = g * lat_dev + r
                at = ((g * lat_dev + r) * levels + level) * half
                for c in range(half):
                    pick[0, at + c, base + columns - half + c] = 1
                    pick[1, at + c, base + c] = 1
    edge_lat = np.repeat(np.arange(lat_rows), levels * half)
    lat = np.concatenate([key_lat, edge_lat, edge_lat])
    low = WIN_LAT * np.arange(windows)[:, None] - WIN_LAT // 2
    inside = (lat[None] >= low) & (lat[None] < low + 2 * WIN_LAT)
    bias = np.where(inside & (lat[None] >= 0), 0.0, MASKED).astype(np.float32)
    return pick, bias[:, None, :], edge


def body(latents, out_grad, qkv_weight, out_weight):
    levels, lat_dev, columns, model_width = latents.shape
    groups = lax.axis_size("head")
    count = lax.axis_size("lon")
    heads = qkv_weight.shape[0]
    width = out_weight.shape[1]
    windows = lat_dev * groups // WIN_LAT
    valid = levels * lat_dev * columns
    block = -(-valid // ROW_TILE) * ROW_TILE
    rows = groups * block
    pick, bias, edge = tables(levels, lat_dev, groups, columns, windows, block)
    keys = rows + 2 * edge
    cols = heads * width
    chips = count // 2
    half = model_width // 2

    lanes = 128
    lane_blocks = half // lanes
    pieces = max(1, chips // lane_blocks)
    dma = pltpu.SemaphoreType.DMA
    shapes = [
        (groups - 1,),
        (groups - 1,),
        (groups - 1,),
        (groups - 1,),
        (2, heads),
        (2, heads),
        (1,),
        (chips - 1,),
        (chips - 1,),
        (chips,),
    ]
    vmem = pl.BlockSpec(memory_space=pltpu.VMEM)
    mixed, latent_grad, qkv = pl.pallas_call(
        functools.partial(kernel, (groups, count, heads, width, block, windows, edge)),
        out_shape=(
            jax.ShapeDtypeStruct(latents.shape, BF16),
            jax.ShapeDtypeStruct(latents.shape, BF16),
            jax.ShapeDtypeStruct((3 * cols, model_width), BF16),
        ),
        in_specs=[vmem] * 6,
        out_specs=(vmem,) * 3,
        scratch_shapes=[
            pltpu.VMEM((rows, model_width), BF16),
            pltpu.VMEM((rows, cols), BF16),
            pltpu.VMEM((groups - 1, block, cols), BF16),
            pltpu.VMEM((heads, rows, width), BF16),
            pltpu.VMEM((heads, keys, 2 * width), BF16),
            pltpu.VMEM((2, heads, edge, 2 * width), BF16),
            pltpu.VMEM((heads, rows, keys), BF16),
            pltpu.VMEM((heads, rows, keys), BF16),
            pltpu.VMEM((2, heads, edge, 2 * width), BF16),
            pltpu.VMEM((2, heads, edge, 2 * width), BF16),
            pltpu.VMEM((heads, rows, 2 * width), F32),
            pltpu.VMEM((rows, cols), BF16),
            pltpu.VMEM((groups, block, cols), BF16),
            pltpu.VMEM((rows, 3 * cols), BF16),
            pltpu.VMEM((2 * lane_blocks, 3 * cols, lanes), BF16),
            pltpu.VMEM((lane_blocks, 3 * cols, lanes), BF16),
            pltpu.VMEM((lane_blocks, 3 * cols, lanes), BF16),
            pltpu.VMEM((chips - 1, 3 * cols // pieces, lanes), BF16),
            pltpu.VMEM((rows, model_width), BF16),
            pltpu.VMEM((groups - 1, block, model_width), BF16),
        ]
        + [dma(s) for s in shapes for _ in range(2)],
        compiler_params=pltpu.CompilerParams(
            collective_id=0, has_side_effects=True, vmem_limit_bytes=56 * 1024 * 1024
        ),
    )(
        latents,
        out_grad,
        qkv_weight.transpose(0, 2, 1).reshape(3 * cols, model_width),
        out_weight.reshape(-1, model_width),
        jnp.asarray(pick, BF16),
        jnp.asarray(bias),
    )
    qkv_grad = qkv.reshape(heads, 3 * width, model_width).transpose(0, 2, 1).astype(F32)
    return mixed, latent_grad, qkv_grad


def solution(mesh):
    placed = (
        P(None, "head", "lon", None),
        P(None, "head", "lon", None),
        P("head", None, None),
        P(),
    )
    return jax.shard_map(
        body,
        mesh=mesh,
        in_specs=placed,
        out_specs=(
            P(None, "head", "lon", None),
            P(None, "head", "lon", None),
            P("head", None, None),
        ),
        check_vma=False,
    )
```

```python
import functools

import jax
import jax.numpy as jnp
import numpy as np
from jax import lax
from jax.experimental import pallas as pl
from jax.experimental.pallas import tpu as pltpu
from jax.sharding import PartitionSpec as P

WIN_LAT = 6
WIN_LON = 8
MASKED = -1e30
ROW_TILE = 16

F32 = jnp.float32
BF16 = jnp.bfloat16


def dot(a, b, dims=(1, 0)):
    return lax.dot_general(
        a, b, (((dims[0],), (dims[1],)), ((), ())), preferred_element_type=F32
    )


def remote(src, dst, sems, index, axis, device):
    send, recv = sems
    return pltpu.make_async_remote_copy(
        src_ref=src,
        dst_ref=dst,
        send_sem=send.at[index],
        recv_sem=recv.at[index],
        device_id={axis: device},
        device_id_type=pl.DeviceIdType.MESH,
    )


def kernel(
    dims,
    lat_ref,
    grad_ref,
    w_in,
    out_w_in,
    pick_ref,
    bias_ref,
    mixed_ref,
    latent_ref,
    qkv_ref,
    w_ref,
    out_w_ref,
    band,
    d_out,
    grad_send,
    query,
    keys,
    halo_send,
    soft,
    hard,
    halo_grad_send,
    halo_grad,
    own_grad,
    attended,
    tokens,
    proj_grad,
    part,
    half_in,
    half_sum,
    chips_in,
    lat_send,
    lat_in,
    *sems,
):
    groups, count, heads, width, block, windows, edge = dims
    levels, lat_dev, columns, depth = lat_ref.shape
    cols = heads * width
    rows = groups * block
    win_rows = rows // windows
    scale = width ** (-0.5)
    gather_s, grad_s, att_s, lat_s, halo_s, hgrad_s, half_s, chip_s, all_s, pair_s = [
        (sems[2 * i], sems[2 * i + 1]) for i in range(10)
    ]
    me = lax.axis_index("lon")
    row = lax.axis_index("head")
    chips = count // 2
    core = lax.rem(me, 2)
    chip = lax.div(me, 2)
    pair = me + 1 - 2 * core
    east = lax.rem(me + 1, count)
    west = lax.rem(me + count - 1, count)
    pending = []

    def partner(d):
        return lax.rem(row + d, groups)

    def chip_at(d):
        return lax.rem(chip + d, chips)

    def block_of(g):
        return pl.ds(pl.multiple_of(g * block, ROW_TILE), block)

    out_w_load = pltpu.make_async_copy(out_w_in, out_w_ref, sems[20].at[0])
    out_w_load.start()
    w_load = pltpu.make_async_copy(w_in, w_ref, sems[20].at[1])
    w_load.start()
    mine = block_of(row)
    def packed(ref):
        parts = [ref[level, r].astype(F32) for r in range(lat_dev) for level in range(levels)]
        if block > len(parts) * columns:
            parts.append(jnp.zeros((block - len(parts) * columns, depth), F32))
        return jnp.concatenate(parts, axis=0).astype(BF16)

    def unpacked(ref, value):
        for r in range(lat_dev):
            for level in range(levels):
                at = (r * levels + level) * columns
                ref[level, r] = value[at : at + columns].astype(BF16)

    offsets = sorted({1, count - 1} | set(range(2, count, 2)))
    barrier = pltpu.get_barrier_semaphore()
    for d in range(1, groups):
        pl.semaphore_signal(
            barrier, inc=1, device_id={"head": partner(d)}, device_id_type=pl.DeviceIdType.MESH
        )
    for d in offsets:
        pl.semaphore_signal(
            barrier,
            inc=1,
            device_id={"lon": lax.rem(me + d, count)},
            device_id_type=pl.DeviceIdType.MESH,
        )
    band[mine, :] = packed(lat_ref)
    pl.semaphore_wait(barrier, groups - 1 + len(offsets))

    def launch(copy):
        copy.start()
        pending.append(copy)
        return copy

    gathers = [
        launch(remote(band.at[mine], band.at[mine], gather_s, d - 1, "head", partner(d)))
        for d in range(1, groups)
    ]
    out_grad = packed(grad_ref)
    out_w_load.wait()
    grads = []
    for d in range(1, groups + 1):
        g = partner(d)
        some = dot(
            out_grad, out_w_ref[pl.ds(pl.multiple_of(g * cols, ROW_TILE), cols), :], (1, 1)
        ).astype(BF16)
        if d < groups:
            grad_send[d - 1] = some
            grads.append(
                launch(remote(grad_send.at[d - 1], d_out.at[mine], grad_s, d - 1, "head", g))
            )
        else:
            d_out[mine, :] = some
    for copy in gathers:
        copy.wait_recv()

    halos = []
    w_load.wait()
    projected = dot(band[...], w_ref[...], (1, 1)).astype(BF16)
    for h in range(heads):
        base = 3 * h * width
        query[h] = (projected[:, base : base + width].astype(F32) * scale).astype(BF16)
        pairs = projected[:, base + width : base + 3 * width]
        keys[h, 0:rows, :] = pairs
        copies = []
        for side, device in ((0, east), (1, west)):
            halo_send[side, h] = dot(pick_ref[side], pairs).astype(BF16)
            copies.append(
                launch(
                    remote(
                        halo_send.at[side, h],
                        keys.at[h, pl.ds(rows + side * edge, edge)],
                        halo_s,
                        (side, h),
                        "lon",
                        device,
                    )
                )
            )
        halos.append(copies)
    for copy in grads:
        copy.wait_recv()

    for copies in halos:
        for copy in copies:
            copy.wait_recv()

    def window(some, w):
        here = pl.ds(pl.multiple_of(w * win_rows, ROW_TILE), win_rows)
        for h in some:
            lanes = slice(h * width, (h + 1) * width)
            k = keys[h, :, 0:width]
            v = keys[h, :, width : 2 * width]
            scores = dot(query[h, here, :], k, (1, 1)) + bias_ref[w]
            prob_grad = dot(d_out[here, lanes], v, (1, 1))
            powers = jnp.exp(scores - jnp.max(scores, axis=-1, keepdims=True))
            probs = powers * (1.0 / jnp.sum(powers, axis=-1, keepdims=True))
            probs_b = probs.astype(BF16)
            hard[h, here, :] = probs_b
            centre = jnp.sum(probs * prob_grad, axis=-1, keepdims=True)
            score_grad = (probs * (prob_grad - centre)).astype(BF16)
            soft[h, here, :] = score_grad
            attended[here, lanes] = dot(probs_b, v).astype(BF16)
            proj_grad[here, 3 * h * width : (3 * h + 1) * width] = (
                dot(score_grad, k) * scale
            ).astype(BF16)

    returns = []
    for first in range(0, heads, 2):
        some = range(first, min(first + 2, heads))
        if windows <= 2:
            for w in range(windows):
                window(some, w)
        else:
            lax.fori_loop(0, windows, lambda w, c, some=some: (window(some, w), c)[1], 0)
        for h in some:
            whole = jnp.concatenate(
                [
                    dot(soft[h], query[h], (0, 0)),
                    dot(hard[h], d_out[:, h * width : (h + 1) * width], (0, 0)),
                ],
                axis=1,
            )
            own_grad[h] = whole[0:rows, :]
            for side in range(2):
                halo_grad_send[side, h] = whole[
                    rows + side * edge : rows + (side + 1) * edge, :
                ].astype(BF16)
        for h in some:
            copies = []
            for side, device in ((0, west), (1, east)):
                copies.append(
                    launch(
                        remote(
                            halo_grad_send.at[side, h],
                            halo_grad.at[side, h],
                            hgrad_s,
                            (side, h),
                            "lon",
                            device,
                        )
                    )
                )
            returns.append(copies)

    sent = []
    for d in range(1, groups):
        sent.append(
            launch(
                remote(
                    attended.at[block_of(partner(d))],
                    tokens.at[row],
                    att_s,
                    d - 1,
                    "head",
                    partner(d),
                )
            )
        )
    tokens[row] = attended[mine, :]

    for h in range(heads):
        for copy in returns[h]:
            copy.wait_recv()
        total = own_grad[h]
        for side in range(2):
            total += dot(pick_ref[side], halo_grad[side, h], (0, 0))
        proj_grad[:, (3 * h + 1) * width : 3 * (h + 1) * width] = total.astype(BF16)

    lanes = part.shape[2]
    lane_blocks = half_in.shape[0]
    wide = 2 * lanes

    def qkv_half(which):
        def one(i, carry):
            at = which * lane_blocks + 2 * i
            found = dot(
                proj_grad[...], band[:, pl.ds(pl.multiple_of(at * lanes, wide), wide)], (0, 0)
            ).astype(BF16)
            part[at] = found[:, :lanes]
            part[at + 1] = found[:, lanes:]
            return carry

        lax.fori_loop(0, lane_blocks // 2, one, 0)

    qkv_half(1 - core)
    halves = launch(
        remote(part.at[pl.ds((1 - core) * lane_blocks, lane_blocks)], half_in, half_s, 0, "lon", pair)
    )
    qkv_half(core)

    def latent(i, carry):
        at = pl.ds(pl.multiple_of(i * wide, wide), wide)
        lat_send[:, at] = dot(proj_grad[...], w_ref[:, at]).astype(BF16)
        return carry

    lax.fori_loop(0, depth // wide, latent, 0)
    lats = [
        launch(
            remote(
                lat_send.at[block_of(partner(d))], lat_in.at[d - 1], lat_s, d - 1, "head", partner(d)
            )
        )
        for d in range(1, groups)
    ]

    halves.wait_recv()
    ours = pl.ds(core * lane_blocks, lane_blocks)
    half_sum[...] = (part[ours].astype(F32) + half_in[...].astype(F32)).astype(BF16)
    piece = chips_in.shape[1]

    def piece_of(t):
        return lax.rem(t, lane_blocks), pl.ds(
            pl.multiple_of(lax.div(t, lane_blocks) * piece, ROW_TILE), piece
        )

    def result_of(t):
        lane, here = piece_of(t)
        at = (core * lane_blocks + lane) * lanes
        return here, pl.ds(pl.multiple_of(at, lanes), lanes)

    exchanged = [
        launch(
            remote(
                half_sum.at[piece_of(chip_at(d))],
                chips_in.at[d - 1],
                chip_s,
                d - 1,
                "lon",
                2 * chip_at(d) + core,
            )
        )
        for d in range(1, chips)
    ]

    for copy in sent:
        copy.wait_recv()
    mixed = jnp.zeros((block, depth), F32)
    for g in range(groups):
        mixed += dot(tokens[g], out_w_ref[g * cols : (g + 1) * cols, :])
    unpacked(mixed_ref, mixed)

    for copy in exchanged:
        copy.wait_recv()
    total = half_sum[piece_of(chip)].astype(F32)
    for d in range(1, chips):
        total += chips_in[d - 1].astype(F32)

    final = result_of(chip)
    qkv_ref[final] = total.astype(BF16)
    spread = [
        launch(
            remote(
                qkv_ref.at[final], qkv_ref.at[final], all_s, d - 1, "lon", 2 * chip_at(d) + core
            )
        )
        for d in range(1, chips)
    ]
    shared = [launch(remote(qkv_ref.at[final], qkv_ref.at[final], pair_s, 0, "lon", pair))]

    for copy in lats:
        copy.wait_recv()
    total = lat_send[mine, :].astype(F32)
    for d in range(1, groups):
        total += lat_in[d - 1].astype(F32)
    unpacked(latent_ref, total)

    for d in range(1, chips):
        spread[d - 1].wait_recv()
        came = result_of(lax.rem(chip + chips - d, chips))
        shared.append(launch(remote(qkv_ref.at[came], qkv_ref.at[came], pair_s, d, "lon", pair)))
    for copy in shared:
        copy.wait_recv()
    for copy in pending:
        copy.wait_send()


def tables(levels, lat_dev, groups, columns, windows, block):
    half = columns // 2
    lat_rows = lat_dev * groups
    edge = lat_rows * levels * half
    pick = np.zeros((2, edge, groups * block), np.float32)
    key_lat = np.full((groups * block,), -(10**6))
    for g in range(groups):
        for r in range(lat_dev):
            for level in range(levels):
                base = g * block + (r * levels + level) * columns
                key_lat[base : base + columns] = g * lat_dev + r
                at = ((g * lat_dev + r) * levels + level) * half
                for c in range(half):
                    pick[0, at + c, base + columns - half + c] = 1
                    pick[1, at + c, base + c] = 1
    edge_lat = np.repeat(np.arange(lat_rows), levels * half)
    lat = np.concatenate([key_lat, edge_lat, edge_lat])
    low = WIN_LAT * np.arange(windows)[:, None] - WIN_LAT // 2
    inside = (lat[None] >= low) & (lat[None] < low + 2 * WIN_LAT)
    bias = np.where(inside & (lat[None] >= 0), 0.0, MASKED).astype(np.float32)
    return pick, bias[:, None, :], edge


def body(latents, out_grad, qkv_weight, out_weight):
    levels, lat_dev, columns, model_width = latents.shape
    groups = lax.axis_size("head")
    count = lax.axis_size("lon")
    heads = qkv_weight.shape[0]
    width = out_weight.shape[1]
    windows = lat_dev * groups // WIN_LAT
    valid = levels * lat_dev * columns
    block = -(-valid // ROW_TILE) * ROW_TILE
    rows = groups * block
    pick, bias, edge = tables(levels, lat_dev, groups, columns, windows, block)
    keys = rows + 2 * edge
    cols = heads * width
    chips = count // 2
    half = model_width // 2

    lanes = 128
    lane_blocks = half // lanes
    pieces = max(1, chips // lane_blocks)
    dma = pltpu.SemaphoreType.DMA
    shapes = [
        (groups - 1,),
        (groups - 1,),
        (groups - 1,),
        (groups - 1,),
        (2, heads),
        (2, heads),
        (1,),
        (chips - 1,),
        (chips - 1,),
        (chips,),
    ]
    vmem = pl.BlockSpec(memory_space=pltpu.VMEM)
    mixed, latent_grad, qkv = pl.pallas_call(
        functools.partial(kernel, (groups, count, heads, width, block, windows, edge)),
        out_shape=(
            jax.ShapeDtypeStruct(latents.shape, BF16),
            jax.ShapeDtypeStruct(latents.shape, BF16),
            jax.ShapeDtypeStruct((3 * cols, model_width), BF16),
        ),
        in_specs=[vmem] * 2 + [pl.BlockSpec(memory_space=pl.ANY)] * 2 + [vmem] * 2,
        out_specs=(vmem,) * 3,
        scratch_shapes=[
            pltpu.VMEM((3 * cols, model_width), BF16),
            pltpu.VMEM((groups * cols, model_width), BF16),
            pltpu.VMEM((rows, model_width), BF16),
            pltpu.VMEM((rows, cols), BF16),
            pltpu.VMEM((groups - 1, block, cols), BF16),
            pltpu.VMEM((heads, rows, width), BF16),
            pltpu.VMEM((heads, keys, 2 * width), BF16),
            pltpu.VMEM((2, heads, edge, 2 * width), BF16),
            pltpu.VMEM((heads, rows, keys), BF16),
            pltpu.VMEM((heads, rows, keys), BF16),
            pltpu.VMEM((2, heads, edge, 2 * width), BF16),
            pltpu.VMEM((2, heads, edge, 2 * width), BF16),
            pltpu.VMEM((heads, rows, 2 * width), F32),
            pltpu.VMEM((rows, cols), BF16),
            pltpu.VMEM((groups, block, cols), BF16),
            pltpu.VMEM((rows, 3 * cols), BF16),
            pltpu.VMEM((2 * lane_blocks, 3 * cols, lanes), BF16),
            pltpu.VMEM((lane_blocks, 3 * cols, lanes), BF16),
            pltpu.VMEM((lane_blocks, 3 * cols, lanes), BF16),
            pltpu.VMEM((chips - 1, 3 * cols // pieces, lanes), BF16),
            pltpu.VMEM((rows, model_width), BF16),
            pltpu.VMEM((groups - 1, block, model_width), BF16),
        ]
        + [dma(s) for s in shapes for _ in range(2)]
        + [dma((2,))],
        compiler_params=pltpu.CompilerParams(
            collective_id=0, has_side_effects=True, vmem_limit_bytes=56 * 1024 * 1024
        ),
    )(
        latents,
        out_grad,
        qkv_weight.transpose(0, 2, 1).reshape(3 * cols, model_width),
        out_weight.reshape(-1, model_width),
        jnp.asarray(pick, BF16),
        jnp.asarray(bias),
    )
    qkv_grad = qkv.reshape(heads, 3 * width, model_width).transpose(0, 2, 1).astype(F32)
    return mixed, latent_grad, qkv_grad


def solution(mesh):
    placed = (
        P(None, "head", "lon", None),
        P(None, "head", "lon", None),
        P("head", None, None),
        P(),
    )
    return jax.shard_map(
        body,
        mesh=mesh,
        in_specs=placed,
        out_specs=(
            P(None, "head", "lon", None),
            P(None, "head", "lon", None),
            P("head", None, None),
        ),
        check_vma=False,
    )
```
